256 devices in a mesh: val: 8 (over z_lo, core), cond: 32 (over z_hi, x, y).
Axes of the slice: x: 4, y: 4, z: 8 (z_hi: 2, z_lo: 4; z = z_hi * 4 + z_lo), core: 2. Of those that a mesh axis runs over, the one named last changes fastest.
Arguments:
- conduction: bfloat16 [2, 512, 96, 9216], P(None, 'cond', 'val'), may hold values from -3 to 3
- valence: bfloat16 [2, 2, 96, 9216], P(None, None, 'val', 'cond'), may hold values from -3 to 3
- resident: bfloat16 [256, 2, 512, 2048], P('val', None, 'cond'), may hold values from -6 to 6
- interaction: float32 [2048], replicated, may hold values from 0.2 to 2
Outputs:
- kernel_row: bfloat16 [256, 2, 512, 2, 512], P('val', None, 'cond')
The draws below stay inside these ranges and needn't reach their ends.
All inputs are finite; a program needn't handle non-finite values.
Results may differ from the reference program's by a relative error of at most 0.005.
Values may be sent and summed in bfloat16 or wider, within the bound.
A program may use at most 128 MiB of HBM per device.

```python
import math
import jax
import jax.numpy as jnp
import numpy as np
from jax import lax

GRID = 96
PLANE = 9216
NC = 512
VN = 2
VR = 256
KXY = 16
KZ = 8
NG = 2048


def shard_levels(rng, extent, shards, least, high):
    def one(position, parts):
        steps = jax.random.uniform(jax.random.fold_in(jax.random.fold_in(rng, 6), position), (parts,), jnp.float32, least / len(shards), high / len(shards))
        return jnp.repeat(jnp.exp(steps), extent[position] // parts).reshape((-1,) + (1,) * (len(extent) - position - 1))

    level = one(*shards[0])
    for cut in shards[1:]:
        level = level * one(*cut)
    return level


def gaussian(key, dims, scale, limit, shards=(), held_as=jnp.bfloat16):
    drawn = jax.random.normal(key, dims, jnp.float32) * scale
    if len(shards) > 0:
        drawn = shard_levels(key, dims, shards, -0.22, 0.18) * drawn
    return jnp.clip(drawn, min=-limit, max=limit).astype(held_as)


def setup_inputs(seed: int = 0) -> dict:
    key_list = jax.random.split(jax.random.key(seed), 5)
    return {
        "conduction": gaussian(key_list[0], (2, NC, GRID, PLANE), 0.5, 3.0, ((1, 32), (2, 8))),
        "valence": gaussian(key_list[1], (2, VN, GRID, PLANE), 0.5, 3.0, ((2, 8), (3, 32))),
        "resident": gaussian(key_list[2], (VR, 2, NC, NG), 1.0, 6.0, ((0, 8), (2, 32))),
        "interaction": jnp.clip(jnp.exp(jax.random.uniform(key_list[3], (NG,), jnp.float32, math.log(0.2), math.log(2.0))), 0.2, 2.0),
    }


def box_indices(kept, points):
    return np.array([g % points for g in range(-(kept // 2), kept // 2)], dtype=np.int32)

def new_densities(conduction, valence, interaction):
    x_index = box_indices(KXY, GRID)
    z_index = box_indices(KZ, GRID)
    val_real = valence[0].astype(jnp.float32).reshape(VN, GRID, GRID, GRID)
    val_imag = valence[1].astype(jnp.float32).reshape(VN, GRID, GRID, GRID)

    def per_band(band_index):
        cond_wave = lax.dynamic_index_in_dim(conduction, band_index, 1, keepdims=False).astype(jnp.float32)
        cond_real = cond_wave[0].reshape(GRID, GRID, GRID)[None]
        cond_imag = cond_wave[1].reshape(GRID, GRID, GRID)[None]
        dens_real = val_real * cond_real + val_imag * cond_imag
        dens_imag = val_real * cond_imag - val_imag * cond_real
        spectrum = jnp.fft.fftn(lax.complex(dens_real, dens_imag), axes=(1, 2, 3), norm='ortho')
        spectrum = jnp.take(spectrum, x_index, axis=1)
        spectrum = jnp.take(spectrum, x_index, axis=2)
        spectrum = jnp.take(spectrum, z_index, axis=3)
        components = jnp.stack([jnp.real(spectrum), jnp.imag(spectrum)], 1).reshape(VN, 2, NG)
        return (components * interaction).astype(jnp.bfloat16)
    scaled = lax.map(per_band, jnp.arange(NC, dtype=jnp.int32))
    return jnp.transpose(scaled, (1, 0, 2, 3)).reshape(VN * NC, 2, NG)

def reference(conduction, valence, resident, interaction):
    scaled = new_densities(conduction, valence, interaction)
    new_real = scaled[:, 0, :].astype(jnp.float32).T
    new_imag = scaled[:, 1, :].astype(jnp.float32).T
    weights_table = jnp.concatenate([jnp.concatenate([new_real, -new_imag], 1), jnp.concatenate([new_imag, new_real], 1)], 0)
    factor = 2.0 / math.sqrt(NG)

    def per_row(band_index):
        resident_row = lax.dynamic_index_in_dim(resident, band_index, 0, keepdims=False).astype(jnp.float32)
        joined = jnp.concatenate([resident_row[0], resident_row[1]], 1)
        kernel = jnp.dot(joined, weights_table, preferred_element_type=jnp.float32, precision=lax.Precision.HIGHEST) * factor
        return jnp.transpose(kernel.reshape(NC, 2, VN, NC), (1, 0, 2, 3)).astype(jnp.bfloat16)
    return lax.map(per_row, jnp.arange(VR, dtype=jnp.int32))
```

```python
import functools
import math

import jax
import jax.numpy as jnp
import ml_dtypes
import numpy as np
from jax import lax
from jax.experimental import pallas as pl
from jax.experimental.pallas import tpu as pltpu
from jax.sharding import PartitionSpec as P

GRID = 96
KXY = 16
KZ = 8
NG = 2048
NZ, NX, NY, NK = 8, 4, 4, 2
CHUNK = 1152
ROWS = 384
F32 = jnp.float32
BF16 = jnp.bfloat16


def split_bf16(a):
    hi = a.astype(ml_dtypes.bfloat16)
    lo = (a - hi.astype(np.float64)).astype(ml_dtypes.bfloat16)
    return hi, lo


@functools.lru_cache(None)
def tables():
    turn = 2.0 * math.pi / GRID
    ky = np.arange(KXY) - KXY // 2
    kz = np.arange(KZ) - KZ // 2
    angle = turn * np.mod(
        np.arange(12)[:, None, None, None] * ky[:, None] + np.arange(GRID)[:, None, None] * kz, GRID
    )
    angle = angle.reshape(CHUNK, KXY * KZ)
    c, s = np.cos(angle), np.sin(angle)
    weights = np.concatenate([np.concatenate([c, -s], 1), np.concatenate([s, c], 1)], 0)
    chunk = np.arange(8)[:, None] * np.repeat(ky, KZ)[None, :] * turn * 12
    chunk_phase = np.stack([np.cos(chunk), np.sin(chunk)], 1).astype(np.float32)
    pair = np.zeros(ROWS, np.int64)
    plane = np.zeros(ROWS, np.int64)
    for w in range(2):
        for quad in range(4):
            for i in range(4):
                base = w * 192 + quad * 48
                p = w * 16 + quad * 4 + i
                pair[base + i * 8 : base + i * 8 + 8] = p
                plane[base + i * 8 : base + i * 8 + 8] = np.arange(8)
                pair[base + 32 + i * 4 : base + 36 + i * 4] = p
                plane[base + 32 + i * 4 : base + 36 + i * 4] = 8 + np.arange(4)
    same = (np.arange(32)[:, None] == pair[None, :]).astype(np.float64)
    kx = np.arange(KXY) - KXY // 2
    ang = turn * np.mod(kx[:, None] * plane[None, :], GRID)
    cx, sx = np.cos(ang)[:, None, :] * same, np.sin(ang)[:, None, :] * same
    planes = np.stack([np.concatenate([cx, sx], 2), np.concatenate([-sx, cx], 2)], 1)
    hi, lo = split_bf16(planes.reshape(KXY * 2 * 32, 2 * ROWS))
    group = np.arange(8)[:, None] * kx[None, :] * turn * 12
    group_phase = np.stack([np.cos(group), np.sin(group)], 1).astype(np.float32)
    group_phase = np.repeat(group_phase[..., None], 128, axis=3)
    return (
        weights.astype(ml_dtypes.bfloat16),
        chunk_phase,
        np.stack([hi, lo], 0),
        group_phase,
    )


class Copies:
    def __init__(self, send, recv):
        self.send, self.recv, self.made = send, recv, []

    def start(self, src, dst, device):
        i = len(self.made)
        copy = pltpu.make_async_remote_copy(
            src_ref=src,
            dst_ref=dst,
            send_sem=self.send.at[i],
            recv_sem=self.recv.at[i],
            device_id=device,
            device_id_type=pl.DeviceIdType.MESH,
        )
        copy.start()
        self.made.append(copy)
        return copy


N_COPIES = 160


def kernel(
    cond_hbm, val_ref, res_hbm, inter_ref, w_hbm, cph_ref, plane_hbm, gph_ref,
    out_ref,
    cond_v, w_v, plane_v, res_v, yblocks, chunks, vals, rho, spec, part, asend, arecv, gath, left, outf,
    local_sem, send_sem, recv_sem,
):
    v = lax.axis_index("val")
    c = lax.axis_index("cond")
    zh, x, y = c // 16, (c // 4) % 4, c % 4
    zl, k = v // 2, v % 2
    z = zh * 4 + zl

    def at(dz=0, dx=0, dy=0, dk=0):
        tz = (z + dz) % NZ
        return {
            "val": (tz % 4) * 2 + (k + dk) % 2,
            "cond": (tz // 4) * 16 + ((x + dx) % NX) * 4 + (y + dy) % NY,
        }

    def in_val(d):
        return {"val": (v + d) % 8, "cond": c}

    copies = Copies(send_sem, recv_sem)

    order = [(h, dx) for h in range(2) for dx in (0, 1, 3, 2)]
    where = [((zh + h) % 2, (x + dx) % NX) for h, dx in order]
    load_cond = []
    load_w = pltpu.make_async_copy(w_hbm, w_v, local_sem.at[8])
    load_w.start()
    for j, (hh, xx) in enumerate(where):
        columns = pl.ds(pl.multiple_of((hh * 4 + xx) * CHUNK, 128), CHUNK)
        load = pltpu.make_async_copy(cond_hbm.at[:, :, :, columns], cond_v.at[j], local_sem.at[j])
        load.start()
        load_cond.append(load)
    load_plane = pltpu.make_async_copy(plane_hbm, plane_v, local_sem.at[9])
    load_plane.start()
    load_res = pltpu.make_async_copy(res_hbm, res_v, local_sem.at[10])
    load_res.start()

    peers = [at(dx=d) for d in (1, 2, 3)] + [at(dy=d) for d in (1, 2, 3)]
    peers += [at(dz=d) for d in range(1, 8)]
    peers += [{"val": ((zl + d) % 4) * 2 + (k + 1) % 2, "cond": c} for d in range(4)]
    barrier = pltpu.get_barrier_semaphore()
    for peer in peers:
        pl.semaphore_signal(barrier, 1, device_id=peer, device_id_type=pl.DeviceIdType.MESH)

    block = val_ref[...].astype(F32)
    rows = [block[p, w, 0:8] for p in range(2) for w in range(2)]
    rows += [block[p, w, 8:12] for p in range(2) for w in range(2)]
    block = jnp.concatenate(rows, axis=0)
    block = jnp.concatenate([block, jnp.zeros((48, 96), F32)], axis=1)
    yblocks[0, y] = block.astype(BF16)
    pl.semaphore_wait(barrier, len(peers))

    own = yblocks.at[0, y]
    from_z = copies.start(own, yblocks.at[1, y], at(dz=4))
    along_y = [[copies.start(own, own, at(dy=d)) for d in (1, 3, 2)]]

    def assemble(h):
        for copy in along_y[h]:
            copy.wait_recv()
        pieces = [yblocks[h, i].astype(F32)[:, :288] for i in range(NY)]
        chunks[h, x] = jnp.concatenate(pieces, axis=1).astype(BF16)
        mine = chunks.at[h, x]
        return [copies.start(mine, mine, at(dx=d)) for d in (1, 3)]

    def pass_on(h, along):
        d = 1 if h == 0 else 3
        there = chunks.at[h, (x + 4 - d) % NX]
        return copies.start(there, there, at(dx=d))

    spec[...] = jnp.zeros_like(spec)

    def transform(j):
        h, _ = order[j]
        hh, xx = where[j]
        load_cond[j].wait()
        vc = chunks[h, xx].astype(F32)
        for p in range(2):
            for w in range(2):
                i = p * 2 + w
                vals[p, w, 0] = vc[i * 8 : i * 8 + 8]
                four = vc[32 + i * 4 : 36 + i * 4]
                vals[p, w, 1] = jnp.concatenate([four, four], axis=0)

        def quad_step(quad, _):
            for lo in range(0, CHUNK, 384):
                lanes = slice(lo, lo + 384)
                cr = cond_v[j, 0, pl.ds(quad * 4, 4), :, lanes].astype(F32)
                ci = cond_v[j, 1, pl.ds(quad * 4, 4), :, lanes].astype(F32)
                cra, cia = cr[:, 0:8], ci[:, 0:8]
                crb = [jnp.concatenate([cr[i, 8:12], cr[i + 1, 8:12]], axis=0) for i in (0, 2)]
                cib = [jnp.concatenate([ci[i, 8:12], ci[i + 1, 8:12]], axis=0) for i in (0, 2)]
                for w in range(2):
                    vr, vi = vals[0, w, 0, :, lanes], vals[1, w, 0, :, lanes]
                    ur, ui = vals[0, w, 1, :, lanes], vals[1, w, 1, :, lanes]
                    real = [vr * cra[i] + vi * cia[i] for i in range(4)]
                    real += [ur * crb[i] + ui * cib[i] for i in range(2)]
                    imag = [vr * cia[i] - vi * cra[i] for i in range(4)]
                    imag += [ur * cib[i] - ui * crb[i] for i in range(2)]
                    at_rows = pl.ds(pl.multiple_of(w * 192 + quad * 48, 16), 48)
                    rho[at_rows, lo : lo + 384] = jnp.concatenate(real, axis=0).astype(BF16)
                    rho[at_rows, CHUNK + lo : CHUNK + lo + 384] = jnp.concatenate(
                        imag, axis=0
                    ).astype(BF16)
            return 0

        lax.fori_loop(0, 4, quad_step, 0)
        new = jnp.dot(rho[...], w_v[...], preferred_element_type=F32)
        phase = cph_ref[hh * 4 + xx]
        co, si = phase[0:1], phase[1:2]
        nr, ni = new[:, :128], new[:, 128:]
        spec[0] += nr * co + ni * si
        spec[1] += ni * co - nr * si

    along_x = [assemble(0)]
    load_w.wait()
    from_z.wait_recv()
    theirs = yblocks.at[1, y]
    along_y.append([copies.start(theirs, theirs, at(dy=d)) for d in (1, 3, 2)])
    transform(0)
    along_x[0][0].wait_recv()
    across = [pass_on(0, along_x[0])]
    along_x.append(assemble(1))
    along_x[0][1].wait_recv()
    transform(1)
    transform(2)
    across[0].wait_recv()
    transform(3)
    transform(4)
    along_x[1][0].wait_recv()
    along_x[1][1].wait_recv()
    across.append(pass_on(1, along_x[1]))
    transform(5)
    transform(6)
    across[1].wait_recv()
    transform(7)

    load_plane.wait()
    both = jnp.concatenate([spec[0], spec[1]], axis=0)
    hi = both.astype(BF16)
    low = (both - hi.astype(F32)).astype(BF16)
    pair = jnp.concatenate([hi, low], axis=1)
    for i in range(4):
        some = slice(i * 256, i * 256 + 256)
        first = jnp.dot(plane_v[0, some, :], pair, preferred_element_type=F32)
        second = jnp.dot(plane_v[1, some, :], hi, preferred_element_type=F32)
        part[some, :] = first[:, :128] + first[:, 128:] + second
    turn = gph_ref[v]
    for i in range(KXY):
        co, si = turn[0, i : i + 1], turn[1, i : i + 1]
        pr = part[i * 64 : i * 64 + 32, :]
        pi = part[i * 64 + 32 : i * 64 + 64, :]
        there = (i % 2) * 64
        asend[i // 2, there : there + 32, :] = (pr * co + pi * si).astype(BF16)
        asend[i // 2, there + 32 : there + 64, :] = (pi * co - pr * si).astype(BF16)
    exchange = []
    for d in range(1, 8):
        exchange.append(copies.start(asend.at[(v + d) % 8], arecv.at[d], in_val(d)))

    load_res.wait()

    def arrange(r, _):
        here = pl.ds(pl.multiple_of(r * 32, 16), 32)
        row = res_v[r]
        turned = jnp.concatenate([row[1], -row[0]], axis=0)
        straight = jnp.concatenate([row[0], row[1]], axis=0)
        for i in range(KXY):
            cols = slice(i * 128, i * 128 + 128)
            to = (i % 2) * 256
            left[i // 2, here, to : to + 128] = straight[:, cols]
            left[i // 2, here, to + 128 : to + 256] = turned[:, cols]
        return 0

    lax.fori_loop(0, 32, arrange, 0)

    total = asend[v].astype(F32)
    for d, copy in enumerate(exchange):
        copy.wait_recv()
        total = total + arecv[d + 1].astype(F32)
    norm = 1.0 / math.sqrt(GRID**3)
    for i in range(2):
        scale = inter_ref[pl.ds(v * 2 + i, 1), :] * norm
        for q in range(2):
            for w in range(2):
                at_row = i * 64 + q * 32 + w * 16
                tile = total[at_row : at_row + 16] * scale
                lanes = slice((i * 2 + q) * 128, (i * 2 + q) * 128 + 128)
                gath[z, k, w, x, y, :, lanes] = tile.astype(BF16)

    every = slice(None)
    lanes_a = slice(0, 128)

    def region(w, lanes, zs=z, xs=x, ys=y):
        return gath.at[zs, k, w, xs, ys, :, lanes]

    def go(ref, **d):
        return copies.start(ref, ref, at(**d))

    to_core = {0: [], 1: []}

    def hand(w, ref):
        to_core[w].append(go(ref, dk=1))

    class Gather:
        def __init__(self, w):
            self.w = w
            cut = 384 if w == 0 else 256
            self.c1, self.c2 = slice(128, cut), slice(cut, 512)

        def one(self):
            w = self.w
            ref = region(w, slice(128, 512))
            self.first = [go(ref, dz=d) for d in (4, 3, 5, 2, 6, 1, 7)]
            ref = region(w, lanes_a)
            axis = "dx" if w == 0 else "dy"
            self.first_a = [go(ref, **{axis: d}) for d in (2, 1, 3)]

        def two(self):
            w = self.w
            for copy in self.first:
                copy.wait_recv()
            r1 = region(w, self.c1, zs=every)
            r2 = region(w, self.c2, zs=every)
            self.second = [go(r1, dx=d) for d in (2, 1, 3)]
            self.second += [go(r2, dy=d) for d in (2, 1, 3)]
            for copy in self.first_a:
                copy.wait_recv()
            if w == 0:
                ra = region(w, lanes_a, xs=every)
                self.second_a = [go(ra, dy=d) for d in (2, 1, 3)]
            else:
                ra = region(w, lanes_a, ys=every)
                self.second_a = [go(ra, dx=d) for d in (2, 1, 3)]

        def three(self):
            w = self.w
            for copy in self.second:
                copy.wait_recv()
            r1 = region(w, self.c1, zs=every, xs=every)
            r2 = region(w, self.c2, zs=every, ys=every)
            self.third = [go(r1, dy=1), go(r1, dy=3), go(r2, dx=1), go(r2, dx=3)]
            for copy in self.second_a:
                copy.wait_recv()
            ra = region(w, lanes_a, xs=every, ys=every)
            self.third_a = [go(ra, dz=1), go(ra, dz=7)]
            hand(w, r1)
            hand(w, r2)
            hand(w, ra)

        def step_a(self, n):
            w = self.w
            self.third_a[0].wait_recv()
            self.third_a[1].wait_recv()
            low, high = (z + 8 - n) % 8, (z + n) % 8
            xl, xh = (every, every) if n < 3 else (slice(0, 2), slice(2, 4))
            right = region(w, lanes_a, zs=low, xs=xl, ys=every)
            leftw = region(w, lanes_a, zs=high, xs=xh, ys=every)
            self.third_a = [go(right, dz=1), go(leftw, dz=7)]
            hand(w, region(w, lanes_a, zs=low, xs=every, ys=every))
            hand(w, region(w, lanes_a, zs=high, xs=every, ys=every))

        def last_a(self):
            w = self.w
            self.third_a[0].wait_recv()
            self.third_a[1].wait_recv()
            hand(w, region(w, lanes_a, zs=(z + 4) % 8, xs=every, ys=every))

        def four(self):
            w = self.w
            ym, yp, xm, xp = (y + 3) % 4, (y + 1) % 4, (x + 3) % 4, (x + 1) % 4
            for copy in self.third:
                copy.wait_recv()
            low, high = slice(0, 4), slice(4, 8)
            self.fourth = [
                go(region(w, self.c1, zs=low, xs=every, ys=ym), dy=1),
                go(region(w, self.c1, zs=high, xs=every, ys=yp), dy=3),
                go(region(w, self.c2, zs=low, xs=xm, ys=every), dx=1),
                go(region(w, self.c2, zs=high, xs=xp, ys=every), dx=3),
            ]
            hand(w, region(w, self.c1, zs=every, xs=every, ys=ym))
            hand(w, region(w, self.c1, zs=every, xs=every, ys=yp))
            hand(w, region(w, self.c2, zs=every, xs=xm, ys=every))
            hand(w, region(w, self.c2, zs=every, xs=xp, ys=every))

        def five(self):
            w = self.w
            for copy in self.fourth:
                copy.wait_recv()
            hand(w, region(w, self.c1, zs=every, xs=every, ys=(y + 2) % 4))
            hand(w, region(w, self.c2, zs=every, xs=(x + 2) % 4, ys=every))

    factor = 2.0 / math.sqrt(NG)

    def multiply(w):
        for copy in to_core[w]:
            copy.wait_recv()

        def block_step(i, _):
            half, m = i // 4, i % 4
            at_rows = pl.ds(pl.multiple_of(m * 256, 256), 256)
            acc = jnp.zeros((256, 256), F32)
            for owner in range(8):
                new = gath[half * 4 + owner // 2, owner % 2, w].reshape(256, 512)
                acc += lax.dot_general(
                    left[owner, at_rows, :],
                    new,
                    (((1,), (1,)), ((), ())),
                    preferred_element_type=F32,
                )
            acc = acc * factor
            for t in range(2):
                start = m * 2048 + (half * 2 + t) * 2 + w
                outf[pl.ds(start, 256, stride=8), :] = acc[:, t * 128 : t * 128 + 128]
            return 0

        lax.fori_loop(0, 8, block_step, 0)

    g0, g1 = Gather(0), Gather(1)
    g0.one()
    g1.one()
    g0.two()
    g1.two()
    g0.three()
    g1.three()
    g0.step_a(1)
    g1.step_a(1)
    g0.four()
    g0.step_a(2)
    g1.step_a(2)
    g1.four()
    g0.step_a(3)
    g1.step_a(3)
    g0.five()
    g0.last_a()
    multiply(0)
    g1.five()
    g1.last_a()
    multiply(1)

    def finish(i, _):
        some = pl.ds(pl.multiple_of(i * 512, 512), 512)
        out_ref[some, :] = outf[some, :].astype(BF16)
        return 0

    lax.fori_loop(0, 16, finish, 0)
    for copy in copies.made:
        copy.wait_send()


def per_device(conduction, valence, resident, interaction):
    weights, chunk_phase, planes, group_phase = (jnp.asarray(t) for t in tables())
    anywhere = pl.BlockSpec(memory_space=pl.ANY)
    vmem = pl.BlockSpec(memory_space=pltpu.VMEM)
    out = pl.pallas_call(
        kernel,
        name="exchange_row",
        out_shape=jax.ShapeDtypeStruct((8192, 128), BF16),
        in_specs=[anywhere, vmem, anywhere, vmem, anywhere, vmem, anywhere, vmem],
        out_specs=vmem,
        scratch_shapes=[
            pltpu.VMEM((8, 2, 16, 12, CHUNK), BF16),
            pltpu.VMEM((2 * CHUNK, 256), BF16),
            pltpu.VMEM((2, 1024, 768), BF16),
            pltpu.VMEM((32, 2, 16, NG), BF16),
            pltpu.VMEM((2, NY, 48, 384), BF16),
            pltpu.VMEM((2, NX, 48, CHUNK), BF16),
            pltpu.VMEM((2, 2, 2, 8, CHUNK), F32),
            pltpu.VMEM((ROWS, 2 * CHUNK), BF16),
            pltpu.VMEM((2, ROWS, 128), F32),
            pltpu.VMEM((1024, 128), F32),
            pltpu.VMEM((8, 128, 128), BF16),
            pltpu.VMEM((8, 128, 128), BF16),
            pltpu.VMEM((NZ, NK, 2, NX, NY, 16, 512), BF16),
            pltpu.VMEM((8, 1024, 512), BF16),
            pltpu.VMEM((8192, 128), F32),
            pltpu.SemaphoreType.DMA((11,)),
            pltpu.SemaphoreType.DMA((N_COPIES,)),
            pltpu.SemaphoreType.DMA((N_COPIES,)),
        ],
        compiler_params=pltpu.CompilerParams(
            collective_id=0, has_side_effects=True, vmem_limit_bytes=56 << 20
        ),
    )(
        conduction,
        valence,
        resident,
        interaction.reshape(KXY, 128),
        weights,
        chunk_phase,
        planes,
        group_phase,
    )
    out = out.reshape(32, 2, 16, 4, 2, 128)
    out = jnp.transpose(out, (0, 1, 2, 4, 3, 5))
    return out.reshape(32, 2, 16, 2, 512)


def solution(mesh):
    in_specs = (
        P(None, "cond", "val", None),
        P(None, None, "val", "cond"),
        P("val", None, "cond", None),
        P(),
    )
    out_specs = P("val", None, "cond", None, None)
    return jax.shard_map(
        per_device, mesh=mesh, in_specs=in_specs, out_specs=out_specs, check_vma=False
    )
```

```python
import functools
import math

import jax
import jax.numpy as jnp
import ml_dtypes
import numpy as np
from jax import lax
from jax.experimental import pallas as pl
from jax.experimental.pallas import tpu as pltpu
from jax.sharding import PartitionSpec as P

GRID = 96
KXY = 16
KZ = 8
NG = 2048
NZ, NX, NY, NK = 8, 4, 4, 2
CHUNK = 1152
ROWS = 384
F32 = jnp.float32
BF16 = jnp.bfloat16


def split_bf16(a):
    hi = a.astype(ml_dtypes.bfloat16)
    lo = (a - hi.astype(np.float64)).astype(ml_dtypes.bfloat16)
    return hi, lo


@functools.lru_cache(None)
def tables():
    turn = 2.0 * math.pi / GRID
    ky = np.arange(KXY) - KXY // 2
    kz = np.arange(KZ) - KZ // 2
    angle = turn * np.mod(
        np.arange(12)[:, None, None, None] * ky[:, None] + np.arange(GRID)[:, None, None] * kz, GRID
    )
    angle = angle.reshape(CHUNK, KXY * KZ)
    c, s = np.cos(angle), np.sin(angle)
    weights = np.concatenate([np.concatenate([c, -s], 1), np.concatenate([s, c], 1)], 0)
    chunk = np.arange(8)[:, None] * np.repeat(ky, KZ)[None, :] * turn * 12
    chunk_phase = np.stack([np.cos(chunk), np.sin(chunk)], 1).astype(np.float32)
    row = np.arange(ROWS)
    pair, plane = row // 192 * 16 + row % 16, row % 192 // 16
    same = (np.arange(32)[:, None] == pair[None, :]).astype(np.float64)
    kx = np.arange(KXY) - KXY // 2
    ang = turn * np.mod(kx[:, None] * plane[None, :], GRID)
    cx, sx = np.cos(ang)[:, None, :] * same, np.sin(ang)[:, None, :] * same
    planes = np.stack([np.concatenate([cx, sx], 2), np.concatenate([-sx, cx], 2)], 1)
    hi, lo = split_bf16(planes.reshape(KXY * 2 * 32, 2 * ROWS))
    group = np.arange(8)[:, None] * kx[None, :] * turn * 12
    group_phase = np.stack([np.cos(group), np.sin(group)], 1).astype(np.float32)
    group_phase = np.repeat(group_phase[..., None], 128, axis=3)
    return (
        weights.astype(ml_dtypes.bfloat16),
        chunk_phase,
        np.stack([hi, lo], 0),
        group_phase,
    )


class Group:
    def __init__(self, send, recv, total, device):
        self.send, self.recv, self.device = send, recv, device
        self.whole = self.describe(total, total, device)

    def describe(self, src, dst, device):
        return pltpu.make_async_remote_copy(
            src_ref=src,
            dst_ref=dst,
            send_sem=self.send,
            recv_sem=self.recv,
            device_id=device,
            device_id_type=pl.DeviceIdType.MESH,
        )

    def start(self, src, dst, device):
        self.describe(src, dst, device).start()

    def wait_recv(self):
        self.whole.wait_recv()

    def wait_send(self):
        self.whole.wait_send()


class Copies:
    def __init__(self, send, recv, device):
        self.send, self.recv, self.device, self.made = send, recv, device, []

    def group(self, total):
        i = len(self.made)
        made = Group(self.send.at[i], self.recv.at[i], total, self.device)
        self.made.append(made)
        return made

    def start(self, src, dst, device):
        made = self.group(src)
        made.start(src, dst, device)
        return made


N_GROUPS = 56


def kernel(
    cond_hbm, val_hbm, res_hbm, inter_hbm, w_hbm, cph_hbm, plane_hbm, gph_hbm,
    out_ref,
    val_ref, inter_ref, cph_ref, gph_ref, cond_v, w_v, plane_v, res_v, yblocks, chunks, vals, rho, spec, part, asend, arecv, gath, left, acc, outf,
    local_sem, send_sem, recv_sem,
):
    v = lax.axis_index("val")
    c = lax.axis_index("cond")
    zh, x, y = c // 16, (c // 4) % 4, c % 4
    zl, k = v // 2, v % 2
    z = zh * 4 + zl

    def at(dz=0, dx=0, dy=0, dk=0):
        tz = (z + dz) % NZ
        return {
            "val": (tz % 4) * 2 + (k + dk) % 2,
            "cond": (tz // 4) * 16 + ((x + dx) % NX) * 4 + (y + dy) % NY,
        }

    def in_val(d):
        return {"val": (v + d) % 8, "cond": c}

    copies = Copies(send_sem, recv_sem, at(dk=1))

    def chunk_at(j):
        i = j % 4
        return j // 4, (x + i + i // 2 - 2 * (i // 3)) % NX

    def load_chunk(j):
        h, xx = chunk_at(j)
        columns = pl.ds(pl.multiple_of(((zh + h) % 2 * 4 + xx) * CHUNK, 128), CHUNK)
        return pltpu.make_async_copy(
            cond_hbm.at[:, :, :, columns], cond_v.at[j], local_sem.at[j]
        )

    load_val = pltpu.make_async_copy(val_hbm, val_ref, local_sem.at[11])
    load_val.start()
    small = [(cph_hbm, cph_ref), (gph_hbm.at[v], gph_ref), (inter_hbm, inter_ref)]
    load_small = [
        pltpu.make_async_copy(src, dst, local_sem.at[12 + i]) for i, (src, dst) in enumerate(small)
    ]
    for load in load_small:
        load.start()
    load_w = pltpu.make_async_copy(w_hbm, w_v, local_sem.at[8])
    load_w.start()
    for j in range(8):
        load_chunk(j).start()
    load_plane = pltpu.make_async_copy(plane_hbm, plane_v, local_sem.at[9])
    load_plane.start()
    load_res = pltpu.make_async_copy(res_hbm, res_v, local_sem.at[10])
    load_res.start()

    plane_peers = [(i, j) for i in (2, 1, 3, 0) for j in (2, 1, 3, 0) if i or j]
    peers = [at(dx=i, dy=j) for i, j in plane_peers]
    peers += [at(dz=d) for d in range(1, 8)]
    peers += [{"val": ((zl + d) % 4) * 2 + (k + 1) % 2, "cond": c} for d in range(4)]
    barrier = pltpu.get_barrier_semaphore()
    for peer in peers:
        pl.semaphore_signal(barrier, 1, device_id=peer, device_id_type=pl.DeviceIdType.MESH)

    load_val.wait()
    block = val_ref[...].astype(F32).reshape(48, 288)
    block = jnp.concatenate([block, jnp.zeros((48, 96), F32)], axis=1)
    yblocks[0, y] = block.astype(BF16)
    pl.semaphore_wait(barrier, len(peers))

    own = yblocks.at[0, y]
    from_z = copies.start(own, yblocks.at[1, y], at(dz=4))
    along_y = [[copies.start(own, own, at(dy=d)) for d in (1, 3, 2)]]

    def assemble(h):
        for copy in along_y[h]:
            copy.wait_recv()
        pieces = [yblocks[h, i].astype(F32)[:, :288] for i in range(NY)]
        chunks[h, x] = jnp.concatenate(pieces, axis=1).astype(BF16)

    one_chunk = chunks.at[0, 0]
    near = {d: copies.group(one_chunk) for d in (1, 3)}
    across = copies.group(one_chunk)
    far = {d: copies.group(one_chunk) for d in (2, 1, 3)}

    spec[...] = jnp.zeros_like(spec)
    acc[...] = jnp.zeros_like(acc)

    def transform(j):
        h, xx = chunk_at(j)
        load_chunk(j).wait()
        vals[...] = chunks[h, xx].astype(F32)

        def plane_step(plane, _):
            at_rows = [pl.ds(pl.multiple_of(w * 192 + plane * 16, 16), 16) for w in range(2)]
            for lo in range(0, CHUNK, 384):
                lanes = slice(lo, lo + 384)
                cr = cond_v[j, 0, plane, :, lanes].astype(F32)
                ci = cond_v[j, 1, plane, :, lanes].astype(F32)
                for w in range(2):
                    vr = vals[pl.ds(plane * 2 + w, 1), lanes]
                    vi = vals[pl.ds(24 + plane * 2 + w, 1), lanes]
                    rho[at_rows[w], lo : lo + 384] = (vr * cr + vi * ci).astype(BF16)
                    rho[at_rows[w], CHUNK + lo : CHUNK + lo + 384] = (vr * ci - vi * cr).astype(BF16)
            return 0

        lax.fori_loop(0, 12, plane_step, 0)
        new = jnp.dot(rho[...], w_v[...], preferred_element_type=F32)
        phase = cph_ref[(zh + h) % 2 * 4 + xx]
        co, si = phase[0:1], phase[1:2]
        nr, ni = new[:, :128], new[:, 128:]
        spec[0] += nr * co + ni * si
        spec[1] += ni * co - nr * si

    assemble(0)
    mine = chunks.at[0, x]
    for d, group in near.items():
        group.start(mine, mine, at(dx=d))
    from_z.wait_recv()
    theirs = yblocks.at[1, y]
    along_y.append([copies.start(theirs, theirs, at(dy=d)) for d in (1, 3, 2)])
    load_w.wait()
    for load in load_small:
        load.wait()

    def chunk_step(j, _):
        @pl.when(j == 1)
        def _():
            near[1].wait_recv()
            passed = chunks.at[0, (x + 3) % NX]
            across.start(passed, passed, at(dx=1))
            assemble(1)
            partners = chunks.at[1, x]
            for d, group in far.items():
                group.start(partners, partners, at(dx=d))
            near[3].wait_recv()

        for place, group in ((3, across), (5, far[3]), (6, far[1]), (7, far[2])):
            pl.when(j == place)(group.wait_recv)
        transform(j)
        return 0

    lax.fori_loop(0, 8, chunk_step, 0)

    load_plane.wait()
    both = jnp.concatenate([spec[0], spec[1]], axis=0)
    hi = both.astype(BF16)
    low = (both - hi.astype(F32)).astype(BF16)
    pair = jnp.concatenate([hi, low], axis=1)

    def plane_rows(i, _):
        some = pl.ds(pl.multiple_of(i * 256, 256), 256)
        first = jnp.dot(plane_v[0, some, :], pair, preferred_element_type=F32)
        second = jnp.dot(plane_v[1, some, :], hi, preferred_element_type=F32)
        part[some, :] = first[:, :128] + first[:, 128:] + second
        return 0

    lax.fori_loop(0, 4, plane_rows, 0)
    turn = gph_ref[...]
    for i in range(KXY):
        co, si = turn[0, i : i + 1], turn[1, i : i + 1]
        pr = part[i * 64 : i * 64 + 32, :]
        pi = part[i * 64 + 32 : i * 64 + 64, :]
        there = (i % 2) * 64
        asend[i // 2, there : there + 32, :] = (pr * co + pi * si).astype(BF16)
        asend[i // 2, there + 32 : there + 64, :] = (pi * co - pr * si).astype(BF16)
    exchange = copies.group(arecv.at[1:8])
    for d in range(1, 8):
        exchange.start(asend.at[(v + d) % 8], arecv.at[d], in_val(d))

    load_res.wait()

    def arrange(r, _):
        here = pl.ds(pl.multiple_of(r * 32, 16), 32)
        row = res_v[r]
        turned = jnp.concatenate([row[1], -row[0]], axis=0)
        straight = jnp.concatenate([row[0], row[1]], axis=0)
        for i in range(KXY):
            cols = slice(i * 128, i * 128 + 128)
            to = (i % 2) * 256
            left[i // 2, here, to : to + 128] = straight[:, cols]
            left[i // 2, here, to + 128 : to + 256] = turned[:, cols]
        return 0

    lax.fori_loop(0, 32, arrange, 0)

    total = asend[v].astype(F32)
    exchange.wait_recv()
    for d in range(1, 8):
        total = total + arecv[d].astype(F32)
    norm = 1.0 / math.sqrt(GRID**3)
    for i in range(2):
        scale = inter_ref[pl.ds(v * 2 + i, 1), :] * norm
        for q in range(2):
            for w in range(2):
                at_row = i * 64 + q * 32 + w * 16
                tile = total[at_row : at_row + 16] * scale
                lanes = slice((i * 2 + q) * 128, (i * 2 + q) * 128 + 128)
                gath[z, k, w, x, y, :, lanes] = tile.astype(BF16)

    every = slice(None)
    lanes_a = slice(0, 128)
    cuts = (384, 256)

    def region(w, lanes, zs, xs, ys):
        return gath.at[zs, k, w, xs, ys, :, lanes]

    def go(group, ref, **d):
        group.start(ref, ref, at(**d))

    def wait_all(some):
        for group in some:
            group.wait_recv()

    def lanes_c(w):
        return slice(128, cuts[w]), slice(cuts[w], 512)

    lanes_both = slice(128, 512)
    halves = (slice(0, 4), slice(4, 8))
    near_two, near_three = slice(0, 2), slice(0, 3)
    hand_a = [copies.group(region(w, lanes_a, every, every, every)) for w in range(2)]
    hand_c = [
        [copies.group(region(w, lanes_both, zs, every, every)) for zs in halves] for w in range(2)
    ]

    def first():
        sends_c = copies.group(region(every, lanes_both, slice(0, 7), x, y))
        ref = region(every, lanes_both, z, x, y)
        for d in (4, 3, 5, 2, 6, 1, 7):
            go(sends_c, ref, dz=d)
        ref = region(every, lanes_a, z, x, y)
        other = copies.group(region(every, lanes_a, z, near_three, every))
        same = copies.group(region(every, lanes_a, z, x, near_three))
        for i, j in plane_peers:
            go(other if i else same, ref, dx=i, dy=j)
        return sends_c, (other, same)

    def second():
        sends = []
        for w in range(2):
            c1, c2 = lanes_c(w)
            g1 = copies.group(region(w, c1, every, near_three, y))
            g2 = copies.group(region(w, c2, every, x, near_three))
            for d in (2, 1, 3):
                go(g1, region(w, c1, every, x, y), dx=d)
                go(g2, region(w, c2, every, x, y), dy=d)
            sends += [g1, g2]
        return sends

    def hand_second():
        for w in range(2):
            c1, c2 = lanes_c(w)
            for h, zs in enumerate(halves):
                go(hand_c[w][h], region(w, c1, zs, every, y), dk=1)
                go(hand_c[w][h], region(w, c2, zs, x, every), dk=1)

    def along_z(n, before):
        after = []
        for w in range(2):
            if n > 1:
                before[w].wait_recv()
            zs, xl, xh = (near_two, every, every) if n < 4 else (0, slice(0, 2), slice(2, 4))
            low, high = (z + 9 - n) % NZ, (z + n - 1) % NZ
            group = copies.group(region(w, lanes_a, zs, every, every))
            go(group, region(w, lanes_a, low, xl, every), dz=1)
            go(group, region(w, lanes_a, high, xh, every), dz=7)
            after.append(group)
            go(hand_a[w], region(w, lanes_a, low, every, every), dk=1)
            if n > 1:
                go(hand_a[w], region(w, lanes_a, high, every, every), dk=1)
        return after

    def end_z(before):
        for w in range(2):
            before[w].wait_recv()
            go(hand_a[w], region(w, lanes_a, (z + 4) % NZ, every, every), dk=1)

    def third(w, h):
        zs = halves[h]
        c1, c2 = lanes_c(w)
        g1 = copies.group(region(w, c1, zs, every, near_two))
        g2 = copies.group(region(w, c2, zs, near_two, every))
        for d in (1, 3):
            go(g1, region(w, c1, zs, every, y), dy=d)
            go(g2, region(w, c2, zs, x, every), dx=d)
        return g1, g2

    def fourth(w, h, before):
        wait_all(before)
        zs = halves[h]
        c1, c2 = lanes_c(w)
        low, high = slice(h * 4, h * 4 + 2), slice(h * 4 + 2, h * 4 + 4)
        ym, yp, xm, xp = (y + 3) % NY, (y + 1) % NY, (x + 3) % NX, (x + 1) % NX
        g1 = copies.group(region(w, c1, zs, every, 0))
        g2 = copies.group(region(w, c2, zs, 0, every))
        go(g1, region(w, c1, low, every, ym), dy=1)
        go(g1, region(w, c1, high, every, yp), dy=3)
        go(g2, region(w, c2, low, xm, every), dx=1)
        go(g2, region(w, c2, high, xp, every), dx=3)
        for i in (ym, yp):
            go(hand_c[w][h], region(w, c1, zs, every, i), dk=1)
        for i in (xm, xp):
            go(hand_c[w][h], region(w, c2, zs, i, every), dk=1)
        return g1, g2

    def fifth(w, h, before):
        wait_all(before)
        zs = halves[h]
        c1, c2 = lanes_c(w)
        go(hand_c[w][h], region(w, c1, zs, every, (y + 2) % NY), dk=1)
        go(hand_c[w][h], region(w, c2, zs, (x + 2) % NX, every), dk=1)

    factor = 2.0 / math.sqrt(NG)

    def multiply(w, h, lanes, planes):
        def step(i, _):
            owners = [(i * planes + j, q) for j in range(planes) for q in range(NK)]
            rows = jnp.concatenate([left[j * NK + q, :, lanes] for j, q in owners], axis=1)
            new = [gath[h * 4 + j, q, w, :, :, :, lanes].reshape(256, -1) for j, q in owners]
            acc[w, h] += lax.dot_general(
                rows,
                jnp.concatenate(new, axis=1),
                (((1,), (1,)), ((), ())),
                preferred_element_type=F32,
            )
            return 0

        lax.fori_loop(0, 4 // planes, step, 0)

    def store(w, h):
        def block_step(m, _):
            at_rows = pl.ds(pl.multiple_of(m * 128, 128), 128)
            for t in range(2):
                start = m * 1024 + (h * 2 + t) * 2 + w
                tile = acc[w, h, at_rows, t * 128 : t * 128 + 128] * factor
                outf[pl.ds(start, 128, stride=8), :] = tile
            return 0

        lax.fori_loop(0, 8, block_step, 0)

    sends_c, sends_a = first()
    wait_all(sends_a)
    steps_a = along_z(1, None)
    sends_c.wait_recv()
    sends_c = second()
    steps_a = along_z(2, steps_a)
    wait_all(sends_c)
    p0, p1, p2 = third(0, 0), third(0, 1), third(1, 0)
    hand_second()
    steps_a = along_z(3, steps_a)
    p0 = fourth(0, 0, p0)
    p3 = third(1, 1)
    p1 = fourth(0, 1, p1)
    steps_a = along_z(4, steps_a)
    p2 = fourth(1, 0, p2)
    fifth(0, 0, p0)
    p3 = fourth(1, 1, p3)
    fifth(0, 1, p1)

    def products(s, _):
        w, h = s // 2, s % 2

        @pl.when(s == 0)
        def _():
            hand_c[0][0].wait_recv()

        @pl.when(s == 1)
        def _():
            fifth(1, 0, p2)
            hand_c[0][1].wait_recv()

        @pl.when(s == 2)
        def _():
            hand_c[1][0].wait_recv()
            hand_a[1].wait_recv()

        @pl.when(s == 3)
        def _():
            hand_c[1][1].wait_recv()

        multiply(w, h, lanes_both, 1)

        @pl.when(s == 0)
        def _():
            end_z(steps_a)
            hand_a[0].wait_recv()

        @pl.when(s == 1)
        def _():
            fifth(1, 1, p3)

        multiply(w, h, lanes_a, 2)
        store(w, h)
        return 0

    lax.fori_loop(0, 4, products, 0)

    def finish(m, _):
        some = pl.ds(pl.multiple_of(m * 1024, 1024), 1024)
        out_ref[some, :] = outf[some, :].astype(BF16)
        return 0

    lax.fori_loop(0, 8, finish, 0)
    for copy in copies.made:
        copy.wait_send()


def write_out(in_ref, out_ref, buf, in_sem, out_sem):
    pieces = [pl.ds(i * 2048, 2048) for i in range(4)]
    loads = [
        pltpu.make_async_copy(in_ref.at[p], buf.at[i], in_sem.at[i]) for i, p in enumerate(pieces)
    ]
    stores = [
        pltpu.make_async_copy(buf.at[i], out_ref.at[p], out_sem.at[i]) for i, p in enumerate(pieces)
    ]
    for load in loads:
        load.start()
    for load, store in zip(loads, stores):
        load.wait()
        store.start()
    for store in stores:
        store.wait()


def per_device(conduction, valence, resident, interaction):
    weights, chunk_phase, planes, group_phase = (jnp.asarray(t) for t in tables())
    anywhere = pl.BlockSpec(memory_space=pl.ANY)
    vmem = pl.BlockSpec(memory_space=pltpu.VMEM)
    out = pl.pallas_call(
        kernel,
        name="exchange_row",
        out_shape=jax.ShapeDtypeStruct((8192, 128), BF16),
        in_specs=[anywhere] * 8,
        out_specs=vmem,
        scratch_shapes=[
            pltpu.VMEM((2, 12, 2, 288), BF16),
            pltpu.VMEM((KXY, 128), F32),
            pltpu.VMEM((8, 2, 128), F32),
            pltpu.VMEM((2, KXY, 128), F32),
            pltpu.VMEM((8, 2, 12, 16, CHUNK), BF16),
            pltpu.VMEM((2 * CHUNK, 256), BF16),
            pltpu.VMEM((2, 1024, 768), BF16),
            pltpu.VMEM((32, 2, 16, NG), BF16),
            pltpu.VMEM((2, NY, 48, 384), BF16),
            pltpu.VMEM((2, NX, 48, CHUNK), BF16),
            pltpu.VMEM((48, CHUNK), F32),
            pltpu.VMEM((ROWS, 2 * CHUNK), BF16),
            pltpu.VMEM((2, ROWS, 128), F32),
            pltpu.VMEM((1024, 128), F32),
            pltpu.VMEM((8, 128, 128), BF16),
            pltpu.VMEM((8, 128, 128), BF16),
            pltpu.VMEM((NZ, NK, 2, NX, NY, 16, 512), BF16),
            pltpu.VMEM((8, 1024, 512), BF16),
            pltpu.VMEM((2, 2, 1024, 256), F32),
            pltpu.VMEM((8192, 128), F32),
            pltpu.SemaphoreType.DMA((15,)),
            pltpu.SemaphoreType.DMA((N_GROUPS,)),
            pltpu.SemaphoreType.DMA((N_GROUPS,)),
        ],
        compiler_params=pltpu.CompilerParams(
            collective_id=0, has_side_effects=True, vmem_limit_bytes=56 << 20
        ),
    )(
        jnp.transpose(conduction, (0, 2, 1, 3)),
        jnp.transpose(valence, (0, 2, 1, 3)),
        resident,
        interaction.reshape(KXY, 128),
        weights,
        chunk_phase,
        planes,
        group_phase,
    )
    out = pl.pallas_call(
        write_out,
        name="write_out",
        out_shape=jax.ShapeDtypeStruct((8192, 128), BF16),
        in_specs=[anywhere],
        out_specs=anywhere,
        scratch_shapes=[
            pltpu.VMEM((4, 2048, 128), BF16),
            pltpu.SemaphoreType.DMA((4,)),
            pltpu.SemaphoreType.DMA((4,)),
        ],
    )(out)
    out = out.reshape(32, 2, 16, 4, 2, 128)
    out = jnp.transpose(out, (0, 1, 2, 4, 3, 5))
    return out.reshape(32, 2, 16, 2, 512)


def solution(mesh):
    in_specs = (
        P(None, "cond", "val", None),
        P(None, None, "val", "cond"),
        P("val", None, "cond", None),
        P(),
    )
    out_specs = P("val", None, "cond", None, None)
    return jax.shard_map(
        per_device, mesh=mesh, in_specs=in_specs, out_specs=out_specs, check_vma=False
    )
```

```python
import functools
import math

import jax
import jax.numpy as jnp
import ml_dtypes
import numpy as np
from jax import lax
from jax.experimental import pallas as pl
from jax.experimental.pallas import tpu as pltpu
from jax.sharding import PartitionSpec as P

GRID = 96
KXY = 16
KZ = 8
NG = 2048
NZ, NX, NY, NK = 8, 4, 4, 2
CHUNK = 1152
ROWS = 384
F32 = jnp.float32
BF16 = jnp.bfloat16


def split_bf16(a):
    hi = a.astype(ml_dtypes.bfloat16)
    lo = (a - hi.astype(np.float64)).astype(ml_dtypes.bfloat16)
    return hi, lo


@functools.lru_cache(None)
def tables():
    turn = 2.0 * math.pi / GRID
    ky = np.arange(KXY) - KXY // 2
    kz = np.arange(KZ) - KZ // 2
    angle = turn * np.mod(
        np.arange(12)[:, None, None, None] * ky[:, None] + np.arange(GRID)[:, None, None] * kz, GRID
    )
    angle = angle.reshape(CHUNK, KXY * KZ)
    c, s = np.cos(angle), np.sin(angle)
    weights = np.concatenate([np.concatenate([c, -s], 1), np.concatenate([s, c], 1)], 0)
    chunk = np.arange(8)[:, None] * np.repeat(ky, KZ)[None, :] * turn * 12
    chunk_phase = np.stack([np.cos(chunk), np.sin(chunk)], 1).astype(np.float32)
    row = np.arange(ROWS)
    pair, plane = row // 192 * 16 + row % 16, row % 192 // 16
    same = (np.arange(32)[:, None] == pair[None, :]).astype(np.float64)
    kx = np.arange(KXY) - KXY // 2
    ang = turn * np.mod(kx[:, None] * plane[None, :], GRID)
    cx, sx = np.cos(ang)[:, None, :] * same, np.sin(ang)[:, None, :] * same
    planes = np.stack([np.concatenate([cx, sx], 2), np.concatenate([-sx, cx], 2)], 1)
    hi, lo = split_bf16(planes.reshape(KXY * 2 * 32, 2 * ROWS))
    group = np.arange(8)[:, None] * kx[None, :] * turn * 12
    group_phase = np.stack([np.cos(group), np.sin(group)], 1).astype(np.float32)
    group_phase = np.repeat(group_phase[..., None], 128, axis=3)
    return (
        weights.astype(ml_dtypes.bfloat16),
        chunk_phase,
        np.stack([hi, lo], 0),
        group_phase,
    )


class Group:
    def __init__(self, send, recv, total, device):
        self.send, self.recv, self.device = send, recv, device
        self.whole = self.describe(total, total, device)

    def describe(self, src, dst, device):
        return pltpu.make_async_remote_copy(
            src_ref=src,
            dst_ref=dst,
            send_sem=self.send,
            recv_sem=self.recv,
            device_id=device,
            device_id_type=pl.DeviceIdType.MESH,
        )

    def start(self, src, dst, device):
        self.describe(src, dst, device).start()

    def wait_recv(self):
        self.whole.wait_recv()

    def wait_send(self):
        self.whole.wait_send()


class Copies:
    def __init__(self, send, recv, device):
        self.send, self.recv, self.device, self.made = send, recv, device, []

    def group(self, total):
        i = len(self.made)
        made = Group(self.send.at[i], self.recv.at[i], total, self.device)
        self.made.append(made)
        return made

    def start(self, src, dst, device):
        made = self.group(src)
        made.start(src, dst, device)
        return made


N_GROUPS = 56


def kernel(
    cond_hbm, val_hbm, res_hbm, inter_hbm, w_hbm, cph_hbm, plane_hbm, gph_hbm,
    out_hbm,
    val_ref, inter_ref, cph_ref, gph_ref, cond_v, w_v, plane_v, res_v, yblocks, chunks, vals, rho, spec, part, asend, arecv, gath, left, outf, out_v,
    local_sem, send_sem, recv_sem,
):
    v = lax.axis_index("val")
    c = lax.axis_index("cond")
    zh, x, y = c // 16, (c // 4) % 4, c % 4
    zl, k = v // 2, v % 2
    z = zh * 4 + zl

    def at(dz=0, dx=0, dy=0, dk=0):
        tz = (z + dz) % NZ
        return {
            "val": (tz % 4) * 2 + (k + dk) % 2,
            "cond": (tz // 4) * 16 + ((x + dx) % NX) * 4 + (y + dy) % NY,
        }

    def in_val(d):
        return {"val": (v + d) % 8, "cond": c}

    copies = Copies(send_sem, recv_sem, at(dk=1))

    def chunk_at(j):
        i = j % 4
        return j // 4, (x + i + i // 2 - 2 * (i // 3)) % NX

    def load_chunk(j):
        h, xx = chunk_at(j)
        columns = pl.ds(pl.multiple_of(((zh + h) % 2 * 4 + xx) * CHUNK, 128), CHUNK)
        return pltpu.make_async_copy(
            cond_hbm.at[:, :, :, columns], cond_v.at[j], local_sem.at[j]
        )

    load_val = pltpu.make_async_copy(val_hbm, val_ref, local_sem.at[11])
    load_val.start()
    small = [(cph_hbm, cph_ref), (gph_hbm.at[v], gph_ref), (inter_hbm, inter_ref)]
    load_small = [
        pltpu.make_async_copy(src, dst, local_sem.at[12 + i]) for i, (src, dst) in enumerate(small)
    ]
    for load in load_small:
        load.start()
    load_w = pltpu.make_async_copy(w_hbm, w_v, local_sem.at[8])
    load_w.start()
    for j in range(8):
        load_chunk(j).start()
    load_plane = pltpu.make_async_copy(plane_hbm, plane_v, local_sem.at[9])
    load_plane.start()
    load_res = pltpu.make_async_copy(res_hbm, res_v, local_sem.at[10])
    load_res.start()

    plane_peers = [(i, j) for i in (2, 1, 3, 0) for j in (2, 1, 3, 0) if i or j]
    peers = [at(dx=i, dy=j) for i, j in plane_peers]
    peers += [at(dz=d) for d in range(1, 8)]
    peers += [{"val": ((zl + d) % 4) * 2 + (k + 1) % 2, "cond": c} for d in range(4)]
    barrier = pltpu.get_barrier_semaphore()
    for peer in peers:
        pl.semaphore_signal(barrier, 1, device_id=peer, device_id_type=pl.DeviceIdType.MESH)

    load_val.wait()
    block = val_ref[...].astype(F32).reshape(48, 288)
    block = jnp.concatenate([block, jnp.zeros((48, 96), F32)], axis=1)
    yblocks[0, y] = block.astype(BF16)
    pl.semaphore_wait(barrier, len(peers))

    own = yblocks.at[0, y]
    from_z = copies.start(own, yblocks.at[1, y], at(dz=4))
    along_y = [[copies.start(own, own, at(dy=d)) for d in (1, 3, 2)]]

    def assemble(h):
        for copy in along_y[h]:
            copy.wait_recv()
        pieces = [yblocks[h, i].astype(F32)[:, :288] for i in range(NY)]
        chunks[h, x] = jnp.concatenate(pieces, axis=1).astype(BF16)

    one_chunk = chunks.at[0, 0]
    near = {d: copies.group(one_chunk) for d in (1, 3)}
    across = copies.group(one_chunk)
    far = {d: copies.group(one_chunk) for d in (2, 1, 3)}

    spec[...] = jnp.zeros_like(spec)

    def transform(j):
        h, xx = chunk_at(j)
        load_chunk(j).wait()
        vals[...] = chunks[h, xx].astype(F32)

        def plane_step(plane, _):
            at_rows = [pl.ds(pl.multiple_of(w * 192 + plane * 16, 16), 16) for w in range(2)]
            for lo in range(0, CHUNK, 384):
                lanes = slice(lo, lo + 384)
                cr = cond_v[j, 0, plane, :, lanes].astype(F32)
                ci = cond_v[j, 1, plane, :, lanes].astype(F32)
                for w in range(2):
                    vr = vals[pl.ds(plane * 2 + w, 1), lanes]
                    vi = vals[pl.ds(24 + plane * 2 + w, 1), lanes]
                    rho[at_rows[w], lo : lo + 384] = (vr * cr + vi * ci).astype(BF16)
                    rho[at_rows[w], CHUNK + lo : CHUNK + lo + 384] = (vr * ci - vi * cr).astype(BF16)
            return 0

        lax.fori_loop(0, 12, plane_step, 0)
        new = jnp.dot(rho[...], w_v[...], preferred_element_type=F32)
        phase = cph_ref[(zh + h) % 2 * 4 + xx]
        co, si = phase[0:1], phase[1:2]
        nr, ni = new[:, :128], new[:, 128:]
        spec[0] += nr * co + ni * si
        spec[1] += ni * co - nr * si

    assemble(0)
    mine = chunks.at[0, x]
    for d, group in near.items():
        group.start(mine, mine, at(dx=d))
    from_z.wait_recv()
    theirs = yblocks.at[1, y]
    along_y.append([copies.start(theirs, theirs, at(dy=d)) for d in (1, 3, 2)])
    load_w.wait()
    for load in load_small:
        load.wait()

    def chunk_step(j, _):
        @pl.when(j == 1)
        def _():
            near[1].wait_recv()
            passed = chunks.at[0, (x + 3) % NX]
            across.start(passed, passed, at(dx=1))
            assemble(1)
            partners = chunks.at[1, x]
            for d, group in far.items():
                group.start(partners, partners, at(dx=d))
            near[3].wait_recv()

        for place, group in ((3, across), (5, far[3]), (6, far[1]), (7, far[2])):
            pl.when(j == place)(group.wait_recv)
        transform(j)
        return 0

    lax.fori_loop(0, 8, chunk_step, 0)

    load_plane.wait()
    both = jnp.concatenate([spec[0], spec[1]], axis=0)
    hi = both.astype(BF16)
    low = (both - hi.astype(F32)).astype(BF16)
    pair = jnp.concatenate([hi, low], axis=1)

    def plane_rows(i, _):
        some = pl.ds(pl.multiple_of(i * 256, 256), 256)
        first = jnp.dot(plane_v[0, some, :], pair, preferred_element_type=F32)
        second = jnp.dot(plane_v[1, some, :], hi, preferred_element_type=F32)
        part[some, :] = first[:, :128] + first[:, 128:] + second
        return 0

    lax.fori_loop(0, 4, plane_rows, 0)
    turn = gph_ref[...]
    for i in range(KXY):
        co, si = turn[0, i : i + 1], turn[1, i : i + 1]
        pr = part[i * 64 : i * 64 + 32, :]
        pi = part[i * 64 + 32 : i * 64 + 64, :]
        there = (i % 2) * 64
        asend[i // 2, there : there + 32, :] = (pr * co + pi * si).astype(BF16)
        asend[i // 2, there + 32 : there + 64, :] = (pi * co - pr * si).astype(BF16)
    exchange = copies.group(arecv.at[1:8])
    for d in range(1, 8):
        exchange.start(asend.at[(v + d) % 8], arecv.at[d], in_val(d))

    load_res.wait()

    def arrange(r, _):
        here = pl.ds(pl.multiple_of(r * 32, 16), 32)
        row = res_v[r]
        turned = jnp.concatenate([row[1], -row[0]], axis=0)
        straight = jnp.concatenate([row[0], row[1]], axis=0)
        for i in range(KXY):
            cols = slice(i * 128, i * 128 + 128)
            to = (i % 2) * 256
            left[i // 2, here, to : to + 128] = straight[:, cols]
            left[i // 2, here, to + 128 : to + 256] = turned[:, cols]
        return 0

    lax.fori_loop(0, 32, arrange, 0)

    total = asend[v].astype(F32)
    exchange.wait_recv()
    for d in range(1, 8):
        total = total + arecv[d].astype(F32)
    norm = 1.0 / math.sqrt(GRID**3)
    for i in range(2):
        scale = inter_ref[pl.ds(v * 2 + i, 1), :] * norm
        for q in range(2):
            for w in range(2):
                at_row = i * 64 + q * 32 + w * 16
                tile = total[at_row : at_row + 16] * scale
                lanes = slice((i * 2 + q) * 128, (i * 2 + q) * 128 + 128)
                gath[z, k, w, x, y, :, lanes] = tile.astype(BF16)

    every = slice(None)
    lanes_a = slice(0, 128)
    cuts = (384, 256)

    def region(w, lanes, zs, xs, ys):
        return gath.at[zs, k, w, xs, ys, :, lanes]

    def go(group, ref, **d):
        group.start(ref, ref, at(**d))

    def wait_all(some):
        for group in some:
            group.wait_recv()

    def lanes_c(w):
        return slice(128, cuts[w]), slice(cuts[w], 512)

    lanes_both = slice(128, 512)
    halves = (slice(0, 4), slice(4, 8))
    near_two, near_three = slice(0, 2), slice(0, 3)
    hand_a = [copies.group(region(w, lanes_a, every, every, every)) for w in range(2)]
    hand_c = [
        [copies.group(region(w, lanes_both, zs, every, every)) for zs in halves] for w in range(2)
    ]

    def first():
        sends_c = copies.group(region(every, lanes_both, slice(0, 7), x, y))
        ref = region(every, lanes_both, z, x, y)
        for d in (4, 3, 5, 2, 6, 1, 7):
            go(sends_c, ref, dz=d)
        ref = region(every, lanes_a, z, x, y)
        other = copies.group(region(every, lanes_a, z, near_three, every))
        same = copies.group(region(every, lanes_a, z, x, near_three))
        for i, j in plane_peers:
            go(other if i else same, ref, dx=i, dy=j)
        return sends_c, (other, same)

    def second():
        sends = []
        for w in range(2):
            c1, c2 = lanes_c(w)
            g1 = copies.group(region(w, c1, every, near_three, y))
            g2 = copies.group(region(w, c2, every, x, near_three))
            for d in (2, 1, 3):
                go(g1, region(w, c1, every, x, y), dx=d)
                go(g2, region(w, c2, every, x, y), dy=d)
            sends += [g1, g2]
        return sends

    def hand_second():
        for w in range(2):
            c1, c2 = lanes_c(w)
            for h, zs in enumerate(halves):
                go(hand_c[w][h], region(w, c1, zs, every, y), dk=1)
                go(hand_c[w][h], region(w, c2, zs, x, every), dk=1)

    def along_z(n, before):
        after = []
        for w in range(2):
            if n > 1:
                before[w].wait_recv()
            zs, xl, xh = (near_two, every, every) if n < 4 else (0, slice(0, 2), slice(2, 4))
            low, high = (z + 9 - n) % NZ, (z + n - 1) % NZ
            group = copies.group(region(w, lanes_a, zs, every, every))
            go(group, region(w, lanes_a, low, xl, every), dz=1)
            go(group, region(w, lanes_a, high, xh, every), dz=7)
            after.append(group)
            go(hand_a[w], region(w, lanes_a, low, every, every), dk=1)
            if n > 1:
                go(hand_a[w], region(w, lanes_a, high, every, every), dk=1)
        return after

    def end_z(before):
        for w in range(2):
            before[w].wait_recv()
            go(hand_a[w], region(w, lanes_a, (z + 4) % NZ, every, every), dk=1)

    def third(w, h):
        zs = halves[h]
        c1, c2 = lanes_c(w)
        g1 = copies.group(region(w, c1, zs, every, near_two))
        g2 = copies.group(region(w, c2, zs, near_two, every))
        for d in (1, 3):
            go(g1, region(w, c1, zs, every, y), dy=d)
            go(g2, region(w, c2, zs, x, every), dx=d)
        return g1, g2

    def fourth(w, h, before):
        wait_all(before)
        zs = halves[h]
        c1, c2 = lanes_c(w)
        low, high = slice(h * 4, h * 4 + 2), slice(h * 4 + 2, h * 4 + 4)
        ym, yp, xm, xp = (y + 3) % NY, (y + 1) % NY, (x + 3) % NX, (x + 1) % NX
        g1 = copies.group(region(w, c1, zs, every, 0))
        g2 = copies.group(region(w, c2, zs, 0, every))
        go(g1, region(w, c1, low, every, ym), dy=1)
        go(g1, region(w, c1, high, every, yp), dy=3)
        go(g2, region(w, c2, low, xm, every), dx=1)
        go(g2, region(w, c2, high, xp, every), dx=3)
        for i in (ym, yp):
            go(hand_c[w][h], region(w, c1, zs, every, i), dk=1)
        for i in (xm, xp):
            go(hand_c[w][h], region(w, c2, zs, i, every), dk=1)
        return g1, g2

    def fifth(w, h, before):
        wait_all(before)
        zs = halves[h]
        c1, c2 = lanes_c(w)
        go(hand_c[w][h], region(w, c1, zs, every, (y + 2) % NY), dk=1)
        go(hand_c[w][h], region(w, c2, zs, (x + 2) % NX, every), dk=1)

    factor = 2.0 / math.sqrt(NG)

    def multiply(s):
        w, h = s // 2, s % 2
        owners = [(i, q) for i in range(4) for q in range(NK)]

        def rows_step(m, _):
            at_rows = pl.ds(pl.multiple_of(m * 512, 512), 512)
            rows = jnp.concatenate([left[i * NK + q, at_rows, :] for i, q in owners], axis=1)
            new = [gath[h * 4 + i, q, w].reshape(256, 512) for i, q in owners]
            product = factor * lax.dot_general(
                rows,
                jnp.concatenate(new, axis=1),
                (((1,), (1,)), ((), ())),
                preferred_element_type=F32,
            )
            for t in range(2):
                start = m * 4096 + (h * 2 + t) * 2 + w
                outf[pl.ds(start, 512, stride=8), :] = product[:, t * 128 : t * 128 + 128]

            @pl.when(s == 3)
            def _():
                def finish(i, _):
                    some = pl.ds(pl.multiple_of(m * 4096 + i * 1024, 1024), 1024)
                    out_v[some, :] = outf[some, :].astype(BF16)
                    return 0

                lax.fori_loop(0, 4, finish, 0)
                write_back(m).start()

            return 0

        lax.fori_loop(0, 2, rows_step, 0)

    def write_back(m):
        some = pl.ds(pl.multiple_of(m * 4096, 4096), 4096)
        return pltpu.make_async_copy(out_v.at[some], out_hbm.at[some], local_sem.at[15 + m])

    sends_c, sends_a = first()
    wait_all(sends_a)
    steps_a = along_z(1, None)
    sends_c.wait_recv()
    sends_c = second()
    steps_a = along_z(2, steps_a)
    wait_all(sends_c)
    p0, p1, p2 = third(0, 0), third(0, 1), third(1, 0)
    hand_second()
    steps_a = along_z(3, steps_a)
    p0 = fourth(0, 0, p0)
    p3 = third(1, 1)
    p1 = fourth(0, 1, p1)
    steps_a = along_z(4, steps_a)
    p2 = fourth(1, 0, p2)
    fifth(0, 0, p0)
    p3 = fourth(1, 1, p3)
    fifth(0, 1, p1)

    end_z(steps_a)

    def products(s, _):
        @pl.when(s == 0)
        def _():
            hand_c[0][0].wait_recv()
            hand_a[0].wait_recv()

        @pl.when(s == 1)
        def _():
            fifth(1, 0, p2)
            hand_c[0][1].wait_recv()

        @pl.when(s == 2)
        def _():
            fifth(1, 1, p3)
            hand_c[1][0].wait_recv()
            hand_a[1].wait_recv()

        @pl.when(s == 3)
        def _():
            hand_c[1][1].wait_recv()

        multiply(s)
        return 0

    lax.fori_loop(0, 4, products, 0)
    for m in range(2):
        write_back(m).wait()
    for copy in copies.made:
        copy.wait_send()


def write_out(in_ref, out_ref, buf, in_sem, out_sem):
    pieces = [pl.ds(i * 2048, 2048) for i in range(4)]
    loads = [
        pltpu.make_async_copy(in_ref.at[p], buf.at[i], in_sem.at[i]) for i, p in enumerate(pieces)
    ]
    stores = [
        pltpu.make_async_copy(buf.at[i], out_ref.at[p], out_sem.at[i]) for i, p in enumerate(pieces)
    ]
    for load in loads:
        load.start()
    for load, store in zip(loads, stores):
        load.wait()
        store.start()
    for store in stores:
        store.wait()


def per_device(conduction, valence, resident, interaction):
    weights, chunk_phase, planes, group_phase = (jnp.asarray(t) for t in tables())
    anywhere = pl.BlockSpec(memory_space=pl.ANY)
    out = pl.pallas_call(
        kernel,
        name="exchange_row",
        out_shape=jax.ShapeDtypeStruct((8192, 128), BF16),
        in_specs=[anywhere] * 8,
        out_specs=anywhere,
        scratch_shapes=[
            pltpu.VMEM((2, 12, 2, 288), BF16),
            pltpu.VMEM((KXY, 128), F32),
            pltpu.VMEM((8, 2, 128), F32),
            pltpu.VMEM((2, KXY, 128), F32),
            pltpu.VMEM((8, 2, 12, 16, CHUNK), BF16),
            pltpu.VMEM((2 * CHUNK, 256), BF16),
            pltpu.VMEM((2, 1024, 768), BF16),
            pltpu.VMEM((32, 2, 16, NG), BF16),
            pltpu.VMEM((2, NY, 48, 384), BF16),
            pltpu.VMEM((2, NX, 48, CHUNK), BF16),
            pltpu.VMEM((48, CHUNK), F32),
            pltpu.VMEM((ROWS, 2 * CHUNK), BF16),
            pltpu.VMEM((2, ROWS, 128), F32),
            pltpu.VMEM((1024, 128), F32),
            pltpu.VMEM((8, 128, 128), BF16),
            pltpu.VMEM((8, 128, 128), BF16),
            pltpu.VMEM((NZ, NK, 2, NX, NY, 16, 512), BF16),
            pltpu.VMEM((8, 1024, 512), BF16),
            pltpu.VMEM((8192, 128), F32),
            pltpu.VMEM((8192, 128), BF16),
            pltpu.SemaphoreType.DMA((17,)),
            pltpu.SemaphoreType.DMA((N_GROUPS,)),
            pltpu.SemaphoreType.DMA((N_GROUPS,)),
        ],
        compiler_params=pltpu.CompilerParams(
            collective_id=0, has_side_effects=True, vmem_limit_bytes=56 << 20
        ),
    )(
        jnp.transpose(conduction, (0, 2, 1, 3)),
        jnp.transpose(valence, (0, 2, 1, 3)),
        resident,
        interaction.reshape(KXY, 128),
        weights,
        chunk_phase,
        planes,
        group_phase,
    )
    out = pl.pallas_call(
        write_out,
        name="write_out",
        out_shape=jax.ShapeDtypeStruct((8192, 128), BF16),
        in_specs=[anywhere],
        out_specs=anywhere,
        scratch_shapes=[
            pltpu.VMEM((4, 2048, 128), BF16),
            pltpu.SemaphoreType.DMA((4,)),
            pltpu.SemaphoreType.DMA((4,)),
        ],
    )(out)
    out = out.reshape(32, 2, 16, 4, 2, 128)
    out = jnp.transpose(out, (0, 1, 2, 4, 3, 5))
    return out.reshape(32, 2, 16, 2, 512)


def solution(mesh):
    in_specs = (
        P(None, "cond", "val", None),
        P(None, None, "val", "cond"),
        P("val", None, "cond", None),
        P(),
    )
    out_specs = P("val", None, "cond", None, None)
    return jax.shard_map(
        per_device, mesh=mesh, in_specs=in_specs, out_specs=out_specs, check_vma=False
    )
```

```python
import functools
import math

import jax
import jax.numpy as jnp
import ml_dtypes
import numpy as np
from jax import lax
from jax.experimental import pallas as pl
from jax.experimental.pallas import tpu as pltpu
from jax.sharding import PartitionSpec as P

GRID = 96
KXY = 16
KZ = 8
NG = 2048
NZ, NX, NY, NK = 8, 4, 4, 2
CHUNK = 1152
ROWS = 384
F32 = jnp.float32
BF16 = jnp.bfloat16


def split_bf16(a):
    hi = a.astype(ml_dtypes.bfloat16)
    lo = (a - hi.astype(np.float64)).astype(ml_dtypes.bfloat16)
    return hi, lo


@functools.lru_cache(None)
def tables():
    turn = 2.0 * math.pi / GRID
    ky = np.arange(KXY) - KXY // 2
    kz = np.arange(KZ) - KZ // 2
    angle = turn * np.mod(
        np.arange(12)[:, None, None, None] * ky[:, None] + np.arange(GRID)[:, None, None] * kz, GRID
    )
    angle = angle.reshape(CHUNK, KXY * KZ)
    c, s = np.cos(angle), np.sin(angle)
    weights = np.concatenate([np.concatenate([c, -s], 1), np.concatenate([s, c], 1)], 0)
    chunk = np.arange(8)[:, None] * np.repeat(ky, KZ)[None, :] * turn * 12
    chunk_phase = np.stack([np.cos(chunk), np.sin(chunk)], 1).astype(np.float32)
    row = np.arange(ROWS)
    pair, plane = row // 192 * 16 + row % 16, row % 192 // 16
    same = (np.arange(32)[:, None] == pair[None, :]).astype(np.float64)
    kx = np.arange(KXY) - KXY // 2
    ang = turn * np.mod(kx[:, None] * plane[None, :], GRID)
    cx, sx = np.cos(ang)[:, None, :] * same, np.sin(ang)[:, None, :] * same
    planes = np.stack([np.concatenate([cx, sx], 2), np.concatenate([-sx, cx], 2)], 1)
    hi, lo = split_bf16(planes.reshape(KXY * 2 * 32, 2 * ROWS))
    group = np.arange(8)[:, None] * kx[None, :] * turn * 12
    group_phase = np.stack([np.cos(group), np.sin(group)], 1).astype(np.float32)
    group_phase = np.repeat(group_phase[..., None], 128, axis=3)
    return (
        weights.astype(ml_dtypes.bfloat16),
        chunk_phase,
        np.stack([hi, lo], 0),
        group_phase,
    )


class Group:
    def __init__(self, send, recv, total, device):
        self.send, self.recv, self.device = send, recv, device
        self.whole = self.describe(total, total, device)

    def describe(self, src, dst, device):
        return pltpu.make_async_remote_copy(
            src_ref=src,
            dst_ref=dst,
            send_sem=self.send,
            recv_sem=self.recv,
            device_id=device,
            device_id_type=pl.DeviceIdType.MESH,
        )

    def start(self, src, dst, device):
        self.describe(src, dst, device).start()

    def wait_recv(self):
        self.whole.wait_recv()

    def wait_send(self):
        self.whole.wait_send()


class Copies:
    def __init__(self, send, recv, device):
        self.send, self.recv, self.device, self.made = send, recv, device, []

    def group(self, total):
        i = len(self.made)
        made = Group(self.send.at[i], self.recv.at[i], total, self.device)
        self.made.append(made)
        return made

    def start(self, src, dst, device):
        made = self.group(src)
        made.start(src, dst, device)
        return made


N_GROUPS = 56


def kernel(
    cond_hbm, val_hbm, res_hbm, inter_hbm, w_hbm, cph_hbm, plane_hbm, gph_hbm,
    out_hbm,
    val_ref, inter_ref, cph_ref, gph_ref, cond_v, w_v, plane_v, res_v, yblocks, chunks, vals, rho, spec, part, asend, arecv, gath, left, outf, out_v,
    local_sem, send_sem, recv_sem,
):
    v = lax.axis_index("val")
    c = lax.axis_index("cond")
    zh, x, y = c // 16, (c // 4) % 4, c % 4
    zl, k = v // 2, v % 2
    z = zh * 4 + zl

    def at(dz=0, dx=0, dy=0, dk=0):
        tz = (z + dz) % NZ
        return {
            "val": (tz % 4) * 2 + (k + dk) % 2,
            "cond": (tz // 4) * 16 + ((x + dx) % NX) * 4 + (y + dy) % NY,
        }

    def in_val(d):
        return {"val": (v + d) % 8, "cond": c}

    copies = Copies(send_sem, recv_sem, at(dk=1))

    plane_peers = [(i, j) for i in (2, 1, 3, 0) for j in (2, 1, 3, 0) if i or j]
    peers = [at(dz=d) for d in (4, 3, 5, 2, 6, 1, 7)]
    peers += [at(dx=i, dy=j) for i, j in plane_peers]
    peers += [{"val": ((zl + d) % 4) * 2 + (k + 1) % 2, "cond": c} for d in range(4)]
    barrier = pltpu.get_barrier_semaphore()
    for peer in peers:
        pl.semaphore_signal(barrier, 1, device_id=peer, device_id_type=pl.DeviceIdType.MESH)

    def chunk_at(j):
        i = j % 4
        return j // 4, (x + i + i // 2 - 2 * (i // 3)) % NX

    def load_chunk(j):
        h, xx = chunk_at(j)
        columns = pl.ds(pl.multiple_of(((zh + h) % 2 * 4 + xx) * CHUNK, 128), CHUNK)
        return pltpu.make_async_copy(
            cond_hbm.at[:, :, :, columns], cond_v.at[j], local_sem.at[j]
        )

    load_val = pltpu.make_async_copy(val_hbm, val_ref, local_sem.at[11])
    load_val.start()
    small = [(cph_hbm, cph_ref), (gph_hbm.at[v], gph_ref), (inter_hbm, inter_ref)]
    load_small = [
        pltpu.make_async_copy(src, dst, local_sem.at[12 + i]) for i, (src, dst) in enumerate(small)
    ]
    for load in load_small:
        load.start()
    load_w = pltpu.make_async_copy(w_hbm, w_v, local_sem.at[8])
    load_w.start()
    for j in range(8):
        load_chunk(j).start()
    load_plane = pltpu.make_async_copy(plane_hbm, plane_v, local_sem.at[9])
    load_plane.start()
    load_res = pltpu.make_async_copy(res_hbm, res_v, local_sem.at[10])
    load_res.start()

    load_val.wait()
    block = val_ref[...].astype(F32).reshape(48, 288)
    block = jnp.concatenate([block, jnp.zeros((48, 96), F32)], axis=1)
    yblocks[0, y] = block.astype(BF16)
    pl.semaphore_wait(barrier, len(peers))

    own = yblocks.at[0, y]
    from_z = copies.start(own, yblocks.at[1, y], at(dz=4))
    along_y = [[copies.start(own, own, at(dy=d)) for d in (1, 3, 2)]]

    def assemble(h):
        for copy in along_y[h]:
            copy.wait_recv()
        pieces = [yblocks[h, i].astype(F32)[:, :288] for i in range(NY)]
        chunks[h, x] = jnp.concatenate(pieces, axis=1).astype(BF16)

    one_chunk = chunks.at[0, 0]
    near = {d: copies.group(one_chunk) for d in (1, 3)}
    across = copies.group(one_chunk)
    far = {d: copies.group(one_chunk) for d in (2, 1, 3)}

    spec[...] = jnp.zeros_like(spec)

    def transform(j):
        h, xx = chunk_at(j)
        load_chunk(j).wait()
        vals[...] = chunks[h, xx].astype(F32)

        def plane_step(plane, _):
            at_rows = [pl.ds(pl.multiple_of(w * 192 + plane * 16, 16), 16) for w in range(2)]
            for lo in range(0, CHUNK, 384):
                lanes = slice(lo, lo + 384)
                cr = cond_v[j, 0, plane, :, lanes].astype(F32)
                ci = cond_v[j, 1, plane, :, lanes].astype(F32)
                for w in range(2):
                    vr = vals[pl.ds(plane * 2 + w, 1), lanes]
                    vi = vals[pl.ds(24 + plane * 2 + w, 1), lanes]
                    rho[at_rows[w], lo : lo + 384] = (vr * cr + vi * ci).astype(BF16)
                    rho[at_rows[w], CHUNK + lo : CHUNK + lo + 384] = (vr * ci - vi * cr).astype(BF16)
            return 0

        lax.fori_loop(0, 12, plane_step, 0)
        new = jnp.dot(rho[...], w_v[...], preferred_element_type=F32)
        phase = cph_ref[(zh + h) % 2 * 4 + xx]
        co, si = phase[0:1], phase[1:2]
        nr, ni = new[:, :128], new[:, 128:]
        spec[0] += nr * co + ni * si
        spec[1] += ni * co - nr * si

    assemble(0)
    mine = chunks.at[0, x]
    for d, group in near.items():
        group.start(mine, mine, at(dx=d))
    from_z.wait_recv()
    theirs = yblocks.at[1, y]
    along_y.append([copies.start(theirs, theirs, at(dy=d)) for d in (1, 3, 2)])
    load_w.wait()
    for load in load_small:
        load.wait()

    def chunk_step(j, _):
        @pl.when(j == 1)
        def _():
            near[1].wait_recv()
            passed = chunks.at[0, (x + 3) % NX]
            across.start(passed, passed, at(dx=1))
            assemble(1)
            partners = chunks.at[1, x]
            for d, group in far.items():
                group.start(partners, partners, at(dx=d))
            near[3].wait_recv()

        for place, group in ((3, across), (5, far[3]), (6, far[1]), (7, far[2])):
            pl.when(j == place)(group.wait_recv)
        transform(j)
        return 0

    lax.fori_loop(0, 8, chunk_step, 0)

    load_plane.wait()
    both = jnp.concatenate([spec[0], spec[1]], axis=0)
    hi = both.astype(BF16)
    low = (both - hi.astype(F32)).astype(BF16)
    pair = jnp.concatenate([hi, low], axis=1)

    def plane_rows(i, _):
        some = pl.ds(pl.multiple_of(i * 256, 256), 256)
        first = jnp.dot(plane_v[0, some, :], pair, preferred_element_type=F32)
        second = jnp.dot(plane_v[1, some, :], hi, preferred_element_type=F32)
        part[some, :] = first[:, :128] + first[:, 128:] + second
        return 0

    lax.fori_loop(0, 4, plane_rows, 0)
    turn = gph_ref[...]
    for i in range(KXY):
        co, si = turn[0, i : i + 1], turn[1, i : i + 1]
        pr = part[i * 64 : i * 64 + 32, :]
        pi = part[i * 64 + 32 : i * 64 + 64, :]
        there = (i % 2) * 64
        asend[i // 2, there : there + 32, :] = (pr * co + pi * si).astype(BF16)
        asend[i // 2, there + 32 : there + 64, :] = (pi * co - pr * si).astype(BF16)
    exchange = copies.group(arecv.at[1:8])
    for d in range(1, 8):
        exchange.start(asend.at[(v + d) % 8], arecv.at[d], in_val(d))

    load_res.wait()

    def arrange(r, _):
        here = pl.ds(pl.multiple_of(r * 32, 16), 32)
        row = res_v[r]
        turned = jnp.concatenate([row[1], -row[0]], axis=0)
        straight = jnp.concatenate([row[0], row[1]], axis=0)
        for i in range(KXY):
            cols = slice(i * 128, i * 128 + 128)
            to = (i % 2) * 256
            left[i // 2, here, to : to + 128] = straight[:, cols]
            left[i // 2, here, to + 128 : to + 256] = turned[:, cols]
        return 0

    lax.fori_loop(0, 32, arrange, 0)

    total = asend[v].astype(F32)
    exchange.wait_recv()
    for d in range(1, 8):
        total = total + arecv[d].astype(F32)
    norm = 1.0 / math.sqrt(GRID**3)
    for i in range(2):
        scale = inter_ref[pl.ds(v * 2 + i, 1), :] * norm
        for q in range(2):
            for w in range(2):
                at_row = i * 64 + q * 32 + w * 16
                tile = total[at_row : at_row + 16] * scale
                lanes = slice((i * 2 + q) * 128, (i * 2 + q) * 128 + 128)
                gath[z, k, w, x, y, :, lanes] = tile.astype(BF16)

    every = slice(None)
    lanes_a = slice(0, 128)
    cuts = (384, 256)

    def region(w, lanes, zs, xs, ys):
        return gath.at[zs, k, w, xs, ys, :, lanes]

    def go(group, ref, **d):
        group.start(ref, ref, at(**d))

    def wait_all(some):
        for group in some:
            group.wait_recv()

    def lanes_c(w):
        return slice(128, cuts[w]), slice(cuts[w], 512)

    lanes_both = slice(128, 512)
    halves = (slice(0, 4), slice(4, 8))
    near_two, near_three = slice(0, 2), slice(0, 3)
    hand_a = [copies.group(region(w, lanes_a, every, every, every)) for w in range(2)]
    hand_c = [
        [copies.group(region(w, lanes_both, zs, every, every)) for zs in halves] for w in range(2)
    ]

    def first():
        sends_c = copies.group(region(every, lanes_both, slice(0, 7), x, y))
        ref = region(every, lanes_both, z, x, y)
        for d in (4, 3, 5, 2, 6, 1, 7):
            go(sends_c, ref, dz=d)
        ref = region(every, lanes_a, z, x, y)
        other = copies.group(region(every, lanes_a, z, near_three, every))
        same = copies.group(region(every, lanes_a, z, x, near_three))
        for i, j in plane_peers:
            go(other if i else same, ref, dx=i, dy=j)
        return sends_c, (other, same)

    def second():
        sends = []
        for w in range(2):
            c1, c2 = lanes_c(w)
            g1 = copies.group(region(w, c1, every, near_three, y))
            g2 = copies.group(region(w, c2, every, x, near_three))
            for d in (2, 1, 3):
                go(g1, region(w, c1, every, x, y), dx=d)
                go(g2, region(w, c2, every, x, y), dy=d)
            sends += [g1, g2]
        return sends

    def hand_second():
        for w in range(2):
            c1, c2 = lanes_c(w)
            for h, zs in enumerate(halves):
                go(hand_c[w][h], region(w, c1, zs, every, y), dk=1)
                go(hand_c[w][h], region(w, c2, zs, x, every), dk=1)

    def along_z(n, before):
        after = []
        for w in range(2):
            if n > 1:
                before[w].wait_recv()
            zs, xl, xh = (near_two, every, every) if n < 4 else (0, slice(0, 2), slice(2, 4))
            low, high = (z + 9 - n) % NZ, (z + n - 1) % NZ
            group = copies.group(region(w, lanes_a, zs, every, every))
            go(group, region(w, lanes_a, low, xl, every), dz=1)
            go(group, region(w, lanes_a, high, xh, every), dz=7)
            after.append(group)
            go(hand_a[w], region(w, lanes_a, low, every, every), dk=1)
            if n > 1:
                go(hand_a[w], region(w, lanes_a, high, every, every), dk=1)
        return after

    def end_z(before):
        for w in range(2):
            before[w].wait_recv()
            go(hand_a[w], region(w, lanes_a, (z + 4) % NZ, every, every), dk=1)

    def third(w, h):
        zs = halves[h]
        c1, c2 = lanes_c(w)
        g1 = copies.group(region(w, c1, zs, every, near_two))
        g2 = copies.group(region(w, c2, zs, near_two, every))
        for d in (1, 3):
            go(g1, region(w, c1, zs, every, y), dy=d)
            go(g2, region(w, c2, zs, x, every), dx=d)
        return g1, g2

    def fourth(w, h, before):
        wait_all(before)
        zs = halves[h]
        c1, c2 = lanes_c(w)
        low, high = slice(h * 4, h * 4 + 2), slice(h * 4 + 2, h * 4 + 4)
        ym, yp, xm, xp = (y + 3) % NY, (y + 1) % NY, (x + 3) % NX, (x + 1) % NX
        g1 = copies.group(region(w, c1, zs, every, 0))
        g2 = copies.group(region(w, c2, zs, 0, every))
        go(g1, region(w, c1, low, every, ym), dy=1)
        go(g1, region(w, c1, high, every, yp), dy=3)
        go(g2, region(w, c2, low, xm, every), dx=1)
        go(g2, region(w, c2, high, xp, every), dx=3)
        for i in (ym, yp):
            go(hand_c[w][h], region(w, c1, zs, every, i), dk=1)
        for i in (xm, xp):
            go(hand_c[w][h], region(w, c2, zs, i, every), dk=1)
        return g1, g2

    def fifth(w, h, before):
        wait_all(before)
        zs = halves[h]
        c1, c2 = lanes_c(w)
        go(hand_c[w][h], region(w, c1, zs, every, (y + 2) % NY), dk=1)
        go(hand_c[w][h], region(w, c2, zs, (x + 2) % NX, every), dk=1)

    factor = 2.0 / math.sqrt(NG)

    def multiply(s):
        w, h = s % 2, s // 2
        owners = [(i, q) for i in range(4) for q in range(NK)]

        rows = jnp.concatenate([left[i * NK + q] for i, q in owners], axis=1)
        new = [gath[h * 4 + i, q, w].reshape(256, 512) for i, q in owners]
        product = factor * lax.dot_general(
            rows,
            jnp.concatenate(new, axis=1),
            (((1,), (1,)), ((), ())),
            preferred_element_type=F32,
        )
        for t in range(2):
            start = (h * 2 + t) * 2 + w
            outf[pl.ds(start, 1024, stride=8), :] = product[:, t * 128 : t * 128 + 128]

    def finish(m, _):
        for i in range(2):
            some = pl.ds(pl.multiple_of(m * 2048 + i * 1024, 1024), 1024)
            out_v[some, :] = outf[some, :].astype(BF16)
        write_back(m).start()
        return 0

    def write_back(m):
        some = pl.ds(pl.multiple_of(m * 2048, 2048), 2048)
        return pltpu.make_async_copy(out_v.at[some], out_hbm.at[some], local_sem.at[15 + m])

    sends_c, sends_a = first()
    wait_all(sends_a)
    steps_a = along_z(1, None)
    sends_c.wait_recv()
    sends_c = second()
    steps_a = along_z(2, steps_a)
    wait_all(sends_c)
    p0, p1, p2 = third(0, 0), third(1, 0), third(0, 1)
    hand_second()
    steps_a = along_z(3, steps_a)
    p0 = fourth(0, 0, p0)
    p3 = third(1, 1)
    p1 = fourth(1, 0, p1)
    steps_a = along_z(4, steps_a)
    p2 = fourth(0, 1, p2)
    fifth(0, 0, p0)
    p3 = fourth(1, 1, p3)
    fifth(1, 0, p1)
    end_z(steps_a)

    def products(s, _):
        @pl.when(s == 0)
        def _():
            hand_c[0][0].wait_recv()
            hand_a[0].wait_recv()

        @pl.when(s == 1)
        def _():
            fifth(0, 1, p2)
            hand_c[1][0].wait_recv()
            hand_a[1].wait_recv()

        @pl.when(s == 2)
        def _():
            fifth(1, 1, p3)
            hand_c[0][1].wait_recv()

        @pl.when(s == 3)
        def _():
            hand_c[1][1].wait_recv()

        multiply(s)
        return 0

    lax.fori_loop(0, 4, products, 0)
    lax.fori_loop(0, 4, finish, 0)
    for m in range(4):
        write_back(m).wait()
    for copy in copies.made:
        copy.wait_send()


def write_out(in_ref, out_ref, buf, in_sem, out_sem):
    pieces = [pl.ds(i * 2048, 2048) for i in range(4)]
    loads = [
        pltpu.make_async_copy(in_ref.at[p], buf.at[i], in_sem.at[i]) for i, p in enumerate(pieces)
    ]
    stores = [
        pltpu.make_async_copy(buf.at[i], out_ref.at[p], out_sem.at[i]) for i, p in enumerate(pieces)
    ]
    for load in loads:
        load.start()
    for load, store in zip(loads, stores):
        load.wait()
        store.start()
    for store in stores:
        store.wait()


def per_device(conduction, valence, resident, interaction):
    weights, chunk_phase, planes, group_phase = (jnp.asarray(t) for t in tables())
    anywhere = pl.BlockSpec(memory_space=pl.ANY)
    out = pl.pallas_call(
        kernel,
        name="exchange_row",
        out_shape=jax.ShapeDtypeStruct((8192, 128), BF16),
        in_specs=[anywhere] * 8,
        out_specs=anywhere,
        scratch_shapes=[
            pltpu.VMEM((2, 12, 2, 288), BF16),
            pltpu.VMEM((KXY, 128), F32),
            pltpu.VMEM((8, 2, 128), F32),
            pltpu.VMEM((2, KXY, 128), F32),
            pltpu.VMEM((8, 2, 12, 16, CHUNK), BF16),
            pltpu.VMEM((2 * CHUNK, 256), BF16),
            pltpu.VMEM((2, 1024, 768), BF16),
            pltpu.VMEM((32, 2, 16, NG), BF16),
            pltpu.VMEM((2, NY, 48, 384), BF16),
            pltpu.VMEM((2, NX, 48, CHUNK), BF16),
            pltpu.VMEM((48, CHUNK), F32),
            pltpu.VMEM((ROWS, 2 * CHUNK), BF16),
            pltpu.VMEM((2, ROWS, 128), F32),
            pltpu.VMEM((1024, 128), F32),
            pltpu.VMEM((8, 128, 128), BF16),
            pltpu.VMEM((8, 128, 128), BF16),
            pltpu.VMEM((NZ, NK, 2, NX, NY, 16, 512), BF16),
            pltpu.VMEM((8, 1024, 512), BF16),
            pltpu.VMEM((8192, 128), F32),
            pltpu.VMEM((8192, 128), BF16),
            pltpu.SemaphoreType.DMA((19,)),
            pltpu.SemaphoreType.DMA((N_GROUPS,)),
            pltpu.SemaphoreType.DMA((N_GROUPS,)),
        ],
        compiler_params=pltpu.CompilerParams(
            collective_id=0, has_side_effects=True, vmem_limit_bytes=56 << 20
        ),
    )(
        jnp.transpose(conduction, (0, 2, 1, 3)),
        jnp.transpose(valence, (0, 2, 1, 3)),
        resident,
        interaction.reshape(KXY, 128),
        weights,
        chunk_phase,
        planes,
        group_phase,
    )
    out = pl.pallas_call(
        write_out,
        name="write_out",
        out_shape=jax.ShapeDtypeStruct((8192, 128), BF16),
        in_specs=[anywhere],
        out_specs=anywhere,
        scratch_shapes=[
            pltpu.VMEM((4, 2048, 128), BF16),
            pltpu.SemaphoreType.DMA((4,)),
            pltpu.SemaphoreType.DMA((4,)),
        ],
    )(out)
    out = out.reshape(32, 2, 16, 4, 2, 128)
    out = jnp.transpose(out, (0, 1, 2, 4, 3, 5))
    return out.reshape(32, 2, 16, 2, 512)


def solution(mesh):
    in_specs = (
        P(None, "cond", "val", None),
        P(None, None, "val", "cond"),
        P("val", None, "cond", None),
        P(),
    )
    out_specs = P("val", None, "cond", None, None)
    return jax.shard_map(
        per_device, mesh=mesh, in_specs=in_specs, out_specs=out_specs, check_vma=False
    )
```
